256 devices in a mesh: tile: 32 (over z, y_hi, core), loop: 8 (over y_lo, x).
Axes of the slice: x: 4, y: 4 (y_hi: 2, y_lo: 2; y = y_hi * 2 + y_lo), z: 8, core: 2. Of those that a mesh axis runs over, the one named last changes fastest.
Arguments:
- echoes: bfloat16 [2, 256, 16384], P(None, 'loop', 'tile'), may hold values from -6 to 6
- interp: bfloat16 [8, 24576, 256], P(None, ('tile', 'loop')), may hold values from -0.375 to 0.375
- offsets: int32 [8, 256], P(None, ('tile', 'loop')), may hold values from -128 to 16256, as said below
- wave: int32 [256], replicated, may hold values from 0 to 16383
- kept: bfloat16 [2048, 96, 128], P(('tile', 'loop')), may hold values from -6 to 6
- lists: int32 [32, 256], P(None, 'loop'), may hold values from 0 to 2047, as said below
Outputs:
- frame: bfloat16 [24576, 32768], P(('tile', 'loop'))
The draws below stay inside these ranges and needn't reach their ends.
Inputs may be any that keep to these rules, and one draw needn't show every extreme that they name: For pulse block b and row group g = t * 8 + l, offsets[b, g] lies within 32 bins of t * 512 + l * 64 + 64 // 2 - 256 // 2. `lists`: row t, entries l * 32 to (l + 1) * 32 - 1 form the list of row group t * 8 + l; each id (o * 8 + l) * 8 + s names slot s of the device at tile index o and the same loop index l. In one list every owner o that appears is named exactly 2 times.
All inputs are finite; a program needn't handle non-finite values.
Results may differ from the reference program's by a relative error of at most 0.005.
Values may be sent and summed in bfloat16 or wider, within the bound.
No kernel may reach another device: no remote copies, remote signals or barrier semaphores. Data moves between devices by JAX's collectives and lax.ppermute only.
A program may use at most 128 MiB of HBM per device.

```python
import math
import jax
import jax.numpy as jnp
from jax import lax

ROWS_DEV = 96
PB_DEV = 32
COLS = 16384
BINS_DEV = 512
RW = 256
DRIFT = 32
CB = 32
KB = 64
CAP = 2
SLOTS = 8
PULSES = 256
PBLOCKS = 8
BINS = 16384
ROWS = 24576
SPAN = 64
HALO = 128
YB = 512
N_TILE = 32
N_LOOP = 8


def draw_offsets(key, part):
    key = jax.random.fold_in(key, 11)
    group_ids = jnp.arange(N_TILE * N_LOOP, dtype=jnp.int32)
    tile_ids = group_ids // N_LOOP
    loop_ids = group_ids % N_LOOP
    centre = tile_ids * BINS_DEV + loop_ids * SPAN + SPAN // 2 - RW // 2
    drifts = jax.random.randint(key, (PBLOCKS, N_TILE * N_LOOP), -DRIFT, DRIFT + 1, dtype=jnp.int32)
    drifts = drifts.at[0, 0].set(-DRIFT).at[0, N_TILE * N_LOOP - 1].set(DRIFT)
    return (centre[None, :] + drifts).astype(jnp.int32)


def draw_lists(key, part):
    key = jax.random.fold_in(key, 23)
    key_hot, key_score, key_order, key_slot = jax.random.split(key, 4)
    hot_level = jax.random.randint(key_hot, (N_TILE,), 0, 4, dtype=jnp.int32)
    scores = jax.random.randint(key_score, (N_TILE, N_LOOP, N_TILE), 0, 1024, dtype=jnp.int32)
    scores = scores + 512 * hot_level[None, None, :]
    forced = jnp.zeros((N_TILE, N_LOOP, N_TILE), jnp.int32)
    forced = forced.at[0, 0, 0].set(8192).at[N_TILE - 1, N_LOOP - 1, N_TILE - 1].set(8192)
    owner_ids = jnp.arange(N_TILE, dtype=jnp.int32)
    scores = (scores + forced) * N_TILE + owner_ids[None, None, :]
    chosen = lax.top_k(scores, CB // CAP)[1].astype(jnp.int32)
    owners = jnp.repeat(chosen, CAP, axis=2)
    shuffle_keys = jax.random.randint(key_order, (N_TILE, N_LOOP, CB), 0, 1 << 20, dtype=jnp.int32) * CB
    shuffle_keys = shuffle_keys + jnp.arange(CB, dtype=jnp.int32)[None, None, :]
    order_ids = jnp.argsort(shuffle_keys, axis=2, stable=True)
    owners = jnp.take_along_axis(owners, order_ids, axis=2)
    slot_ids = jax.random.randint(key_slot, (N_TILE, N_LOOP, CB), 0, SLOTS, dtype=jnp.int32)
    slot_ids = slot_ids.at[0, 0].set(jnp.where(owners[0, 0] == 0, 0, slot_ids[0, 0]))
    slot_ids = slot_ids.at[N_TILE - 1, N_LOOP - 1].set(jnp.where(owners[N_TILE - 1, N_LOOP - 1] == N_TILE - 1, SLOTS - 1, slot_ids[N_TILE - 1, N_LOOP - 1]))
    loop_ids = jnp.arange(N_LOOP, dtype=jnp.int32)[None, :, None]
    block_ids = (owners * N_LOOP + loop_ids) * SLOTS + slot_ids
    return block_ids.reshape(N_TILE, N_LOOP * CB).astype(jnp.int32)


def set_ends(entries, own_key, least, high):
    extent = entries.shape
    spot = [jax.random.randint(jax.random.fold_in(own_key, axis), (), 0, extent[axis]) for axis in range(len(extent))]
    entries = entries.at[tuple(spot)].set(least)
    longest = extent.index(max(extent))
    spot[longest] = (spot[longest] + 1) % extent[longest]
    return entries.at[tuple(spot)].set(high)


def shard_levels(stream_key, dims, cuts, low, high):
    gain, own = 1.0, jax.random.fold_in(stream_key, 6)
    for position, shards_of in cuts:
        draws = jnp.exp(jax.random.uniform(jax.random.fold_in(own, position), (shards_of,), jnp.float32, low / len(cuts), high / len(cuts)))
        gain = gain * jnp.repeat(draws, dims[position] // shards_of).reshape([-1 if axis == position else 1 for axis in range(len(dims))])
    return gain


def normal_values(key, dims, scale, limit, cuts=(), kind=jnp.bfloat16):
    gain = shard_levels(key, dims, cuts, -0.22, 0.18) if cuts else 1.0
    entries = jax.random.normal(key, dims, jnp.float32) * scale * gain
    return jnp.minimum(jnp.maximum(entries, -limit), limit).astype(kind)


def setup_inputs(seed: int = 0) -> dict:
    keys = jax.random.split(jax.random.key(seed), 7)
    echoes = normal_values(keys[0], (2, PULSES, BINS), 1.0, 6.0, ((1, 8), (2, 32)))
    interp = normal_values(keys[1], (PBLOCKS, ROWS, RW), RW ** -0.5, 0.375, ((1, 256),))
    offsets = draw_offsets(jax.random.fold_in(keys[6], 71), 0)
    wave = set_ends(jax.random.randint(keys[3], (PULSES,), 0, COLS), jax.random.fold_in(keys[3], 1), 0, COLS - 1).astype(jnp.int32)
    kept = normal_values(keys[4], (N_TILE * N_LOOP * SLOTS, ROWS_DEV, 2 * KB), 1.0, 6.0, ((0, 256),))
    lists = draw_lists(jax.random.fold_in(keys[6], 71), 0)
    return dict(echoes=echoes, interp=interp, offsets=offsets, wave=wave, kept=kept, lists=lists)


def steering_rows(wave_rows, col_count):
    column_ids = jnp.arange(col_count, dtype=jnp.int32)
    phases = (wave_rows[:, None] * column_ids[None, :] % col_count).astype(jnp.float32) * (2.0 * math.pi / col_count)
    cosine = jnp.cos(phases).astype(jnp.bfloat16)
    sine_part = jnp.sin(phases).astype(jnp.bfloat16)
    top_rows = jnp.concatenate([cosine, sine_part], axis=1)
    low_rows = jnp.concatenate([-sine_part, cosine], axis=1)
    return jnp.concatenate([top_rows, low_rows], axis=0)

def upsample_table(coarse, fine):
    factor = fine // coarse
    fine_ids = jnp.arange(fine, dtype=jnp.int32)
    lower_ids = fine_ids // factor
    upper_ids = jnp.minimum(lower_ids + 1, coarse - 1)
    fraction = (fine_ids % factor).astype(jnp.float32) / factor
    coarse_ids = jnp.arange(coarse, dtype=jnp.int32)[:, None]
    up_table = jnp.where(coarse_ids == lower_ids[None, :], 1.0 - fraction[None, :], 0.0)
    up_table = up_table + jnp.where(coarse_ids == upper_ids[None, :], fraction[None, :], 0.0)
    return up_table.astype(jnp.bfloat16)

def reference(echoes, interp, offsets, wave, kept, lists):
    padded = jnp.pad(echoes, ((0, 0), (0, 0), (HALO, HALO)))
    steering = jnp.concatenate([steering_rows(wave[block_id * PB_DEV:(block_id + 1) * PB_DEV], COLS) for block_id in range(PBLOCKS)], axis=0).astype(jnp.float32)
    up_table = upsample_table(KB, YB).astype(jnp.float32)
    scaling = 1.0 / math.sqrt(PULSES)

    def row_group(group_id):
        tile_index = group_id // N_LOOP
        loop_index = group_id % N_LOOP
        pieces = []
        for block_id in range(PBLOCKS):
            first_bin = (offsets[block_id, group_id] + HALO).astype(jnp.int32)
            samples = lax.dynamic_slice(padded, (jnp.int32(0), jnp.int32(block_id * PB_DEV), first_bin), (2, PB_DEV, RW))
            samples = samples.reshape(2 * PB_DEV, RW)
            weights = lax.dynamic_slice(interp[block_id], ((group_id * ROWS_DEV).astype(jnp.int32), jnp.int32(0)), (ROWS_DEV, RW))
            pieces.append(jnp.dot(weights, samples.T, preferred_element_type=jnp.float32).astype(jnp.bfloat16))
        mixed_rows = jnp.concatenate(pieces, axis=1).astype(jnp.float32)
        image_sum = jnp.dot(mixed_rows, steering, precision=lax.Precision.HIGHEST) * scaling
        block_ids = lax.dynamic_slice(lists[tile_index], ((loop_index * CB).astype(jnp.int32),), (CB,))
        blocks = kept[block_ids].astype(jnp.float32)
        real_part = jnp.einsum('cxk,kj->xcj', blocks[:, :, :KB], up_table, precision=lax.Precision.HIGHEST).reshape(ROWS_DEV, COLS)
        imag_part = jnp.einsum('cxk,kj->xcj', blocks[:, :, KB:], up_table, precision=lax.Precision.HIGHEST).reshape(ROWS_DEV, COLS)
        return (image_sum + jnp.concatenate([real_part, imag_part], axis=1)).astype(jnp.bfloat16)
    frames = lax.map(row_group, jnp.arange(N_TILE * N_LOOP, dtype=jnp.int32))
    return frames.reshape(ROWS, 2 * COLS)
```

```python
import math

import jax
import jax.numpy as jnp
from jax import lax
from jax.experimental import pallas as pl
from jax.experimental.pallas import tpu as pltpu
from jax.sharding import PartitionSpec as P

COLS = 16384
DRIFT = 32
NAMED = 2
LANES = 128
STEPS = 16
FINE = 1024


def upsample_table(coarse, fine):
    factor = fine // coarse
    fine_ids = jnp.arange(fine, dtype=jnp.int32)
    lower_ids = fine_ids // factor
    upper_ids = jnp.minimum(lower_ids + 1, coarse - 1)
    fraction = (fine_ids % factor).astype(jnp.float32) / factor
    coarse_ids = jnp.arange(coarse, dtype=jnp.int32)[:, None]
    up_table = jnp.where(coarse_ids == lower_ids[None, :], 1.0 - fraction[None, :], 0.0)
    up_table = up_table + jnp.where(coarse_ids == upper_ids[None, :], fraction[None, :], 0.0)
    return up_table.astype(jnp.bfloat16)


def turn(wave, column_ids):
    phase = (wave[:, None] * column_ids[None, :] % COLS).astype(jnp.float32) * (2.0 * math.pi / COLS)
    return jnp.cos(phase), jnp.sin(phase)


def select_kernel(pick_ref, kept_ref, out_ref, sems):
    count = out_ref.shape[0]
    copies = [
        pltpu.make_async_copy(kept_ref.at[pick_ref[i]], out_ref.at[i], sems.at[i])
        for i in range(count)
    ]
    for copy in copies:
        copy.start()
    for copy in copies:
        copy.wait()


def select_blocks(pick, kept):
    count = pick.shape[0]
    return pl.pallas_call(
        select_kernel,
        grid_spec=pltpu.PrefetchScalarGridSpec(
            num_scalar_prefetch=1,
            grid=(),
            in_specs=[pl.BlockSpec(memory_space=pltpu.VMEM)],
            out_specs=pl.BlockSpec(memory_space=pl.ANY),
            scratch_shapes=[pltpu.SemaphoreType.DMA((count,))],
        ),
        out_shape=jax.ShapeDtypeStruct((count,) + kept.shape[1:], kept.dtype),
        name="select_blocks",
    )(pick, kept)


def image_kernel(first_ref, got_ref, interp_ref, near_cos, near_sin, far_cos, far_sin, out_ref, mixed):
    blocks, rows, window = interp_ref.shape
    pulses = got_ref.shape[1] // 2
    span = got_ref.shape[2]
    for b in range(blocks):
        samples = got_ref[b].astype(jnp.float32)
        samples = pltpu.roll(samples, span - first_ref[b], 1)[:, :window].astype(jnp.bfloat16)
        product = lax.dot_general(
            interp_ref[b], samples, (((1,), (1,)), ((), ())), preferred_element_type=jnp.float32
        ).astype(jnp.bfloat16)
        mixed[0:rows, b * pulses:(b + 1) * pulses] = product[:, :pulses]
        mixed[rows:2 * rows, b * pulses:(b + 1) * pulses] = product[:, pulses:]
    scaling = 1.0 / math.sqrt(blocks * pulses)
    wide = 2 * LANES

    def step(j, carry):
        for part in range(FINE // wide):
            cosines, sines = [], []
            for half in range(2):
                k = part * 2 + half
                turn_cos = far_cos[j, :, k:k + 1]
                turn_sin = far_sin[j, :, k:k + 1]
                cosines.append((turn_cos * near_cos[...] - turn_sin * near_sin[...]).astype(jnp.bfloat16))
                sines.append((turn_sin * near_cos[...] + turn_cos * near_sin[...]).astype(jnp.bfloat16))
            by_cos = jnp.dot(mixed[...], jnp.concatenate(cosines, 1), preferred_element_type=jnp.float32)
            by_sin = jnp.dot(mixed[...], jnp.concatenate(sines, 1), preferred_element_type=jnp.float32)
            columns = slice(part * wide, (part + 1) * wide)
            out_ref[j, :, columns] = (by_cos[:rows] - by_sin[rows:]) * scaling
            out_ref[STEPS + j, :, columns] = (by_sin[:rows] + by_cos[rows:]) * scaling
        return carry

    lax.fori_loop(0, STEPS, step, 0)


def image_of(first, got, interp, near, far):
    rows = interp.shape[1]
    vmem = pl.BlockSpec(memory_space=pltpu.VMEM)
    return pl.pallas_call(
        image_kernel,
        grid_spec=pltpu.PrefetchScalarGridSpec(
            num_scalar_prefetch=1,
            grid=(),
            in_specs=[vmem] * 6,
            out_specs=vmem,
            scratch_shapes=[pltpu.VMEM((2 * rows, got.shape[0] * got.shape[1] // 2), jnp.bfloat16)],
        ),
        out_shape=pltpu.VMEM((2 * STEPS, rows, FINE), jnp.float32),
        compiler_params=pltpu.CompilerParams(vmem_limit_bytes=24 * 1024 * 1024),
        cost_estimate=pl.CostEstimate(
            flops=4 * rows * 256 * 2 * COLS, bytes_accessed=20 * 1024 * 1024, transcendentals=0
        ),
        name="image_rows",
    )(first, got, interp, *near, *far)


def frame_kernel(place_ref, recv_ref, table_ref, image_ref, out_ref):
    s = pl.program_id(0)
    per_step = out_ref.shape[1] // table_ref.shape[2]
    fine = table_ref.shape[2]
    rows = out_ref.shape[0]
    base = (s % STEPS) * per_step
    coarse = jnp.concatenate([recv_ref[place_ref[base + i]] for i in range(per_step)], 0)
    kept_part = jnp.dot(coarse, table_ref[s // STEPS], preferred_element_type=jnp.float32)
    for i in range(per_step):
        columns = slice(i * fine, (i + 1) * fine)
        out_ref[:, columns] = (
            image_ref[s, :, columns] + kept_part[i * rows:(i + 1) * rows]
        ).astype(jnp.bfloat16)


def frame_of(place, recv, tables, image):
    rows = recv.shape[1]
    vmem = pl.BlockSpec(memory_space=pltpu.VMEM)
    return pl.pallas_call(
        frame_kernel,
        grid_spec=pltpu.PrefetchScalarGridSpec(
            num_scalar_prefetch=1,
            grid=(2 * STEPS,),
            in_specs=[vmem] * 3,
            out_specs=pl.BlockSpec((rows, FINE), lambda s, place: (0, s)),
        ),
        out_shape=jax.ShapeDtypeStruct((rows, 2 * COLS), jnp.bfloat16),
        compiler_params=pltpu.CompilerParams(vmem_limit_bytes=16 * 1024 * 1024),
        name="frame_rows",
    )(place, recv, tables, image)


def body(echoes, interp, offsets, wave, kept, lists):
    tiles = lax.axis_size("tile")
    loops = lax.axis_size("loop")
    my_tile = lax.axis_index("tile")
    my_loop = lax.axis_index("loop")
    slots, rows, samples = kept.shape
    count = lists.shape[1]
    pulse_block, bins_dev = echoes.shape[1:]
    window = interp.shape[2]
    bin_span = bins_dev // loops
    rim = window // 2 - bin_span // 2 + DRIFT

    owners = lists // (slots * loops)
    order = jnp.arange(count, dtype=jnp.int32)[None, :] * slots + lists % slots
    mine = owners == my_tile
    least = jnp.min(jnp.where(mine, order, count * slots), axis=1) % slots
    last = jnp.max(jnp.where(mine, order, 0), axis=1) % slots
    pick = jnp.stack([least, last], axis=1).reshape(tiles * NAMED)
    send = select_blocks(pick, kept).reshape(tiles, NAMED, rows, samples)
    recv = lax.all_to_all(send, "tile", 0, 0, tiled=True).reshape(tiles * NAMED, rows, samples)

    ends = tiles - 1
    before = lax.ppermute(echoes[:, :, bins_dev - rim:], "tile", [(i, i + 1) for i in range(ends)])
    after = lax.ppermute(echoes[:, :, :rim], "tile", [(i + 1, i) for i in range(ends)])
    extended = jnp.concatenate([before, echoes, after], axis=2).reshape(2 * pulse_block, bins_dev + 2 * rim)
    reach = 3 * LANES
    starts = [i * bin_span // LANES * LANES for i in range(loops)]
    outgoing = jnp.stack([extended[:, start:start + reach] for start in starts], axis=0)
    got = lax.all_to_all(outgoing, "loop", 0, 0, tiled=True)
    first = offsets[:, 0] - (my_tile * bins_dev - rim + my_loop * bin_span // LANES * LANES)

    near = turn(wave, jnp.arange(LANES, dtype=jnp.int32))
    far = turn(wave, jnp.arange(LANES, dtype=jnp.int32) * LANES)
    far = [x.reshape(-1, STEPS, LANES // STEPS).transpose(1, 0, 2) for x in far]
    image = image_of(first, got, interp, near, far)

    my_owners = lax.dynamic_index_in_dim(owners, my_tile, 0, keepdims=False)
    ids = jnp.arange(count, dtype=jnp.int32)
    earlier = (my_owners[:, None] == my_owners[None, :]) & (ids[None, :] < ids[:, None])
    place = my_owners * NAMED + jnp.any(earlier, axis=1).astype(jnp.int32)
    table = upsample_table(samples // 2, COLS // count)
    blank = jnp.zeros_like(table)
    tables = jnp.stack([jnp.concatenate([table, blank], 0), jnp.concatenate([blank, table], 0)], 0)
    return frame_of(place, recv, tables, image)


def solution(mesh):
    placed = (
        P(None, "loop", "tile"),
        P(None, ("tile", "loop"), None),
        P(None, ("tile", "loop")),
        P(),
        P(("tile", "loop"), None, None),
        P(None, "loop"),
    )
    return jax.shard_map(
        body, mesh=mesh, in_specs=placed, out_specs=P(("tile", "loop"), None), check_vma=False
    )
```

```python
import math

import jax
import jax.numpy as jnp
from jax import lax
from jax.experimental import pallas as pl
from jax.experimental.pallas import tpu as pltpu
from jax.sharding import PartitionSpec as P

COLS = 16384
DRIFT = 32
NAMED = 2
LANES = 128
STEPS = 16
FINE = 1024
QUARTERS = 4


def upsample_table(coarse, fine):
    factor = fine // coarse
    fine_ids = jnp.arange(fine, dtype=jnp.int32)
    lower_ids = fine_ids // factor
    upper_ids = jnp.minimum(lower_ids + 1, coarse - 1)
    fraction = (fine_ids % factor).astype(jnp.float32) / factor
    coarse_ids = jnp.arange(coarse, dtype=jnp.int32)[:, None]
    up_table = jnp.where(coarse_ids == lower_ids[None, :], 1.0 - fraction[None, :], 0.0)
    up_table = up_table + jnp.where(coarse_ids == upper_ids[None, :], fraction[None, :], 0.0)
    return up_table.astype(jnp.bfloat16)


def turn(wave, column_ids):
    phase = (wave[:, None] * column_ids[None, :] % COLS).astype(jnp.float32) * (2.0 * math.pi / COLS)
    return jnp.cos(phase), jnp.sin(phase)


def select_kernel(least_ref, last_ref, kept_ref, out_ref):
    for i in range(out_ref.shape[0] // NAMED):
        out_ref[NAMED * i] = kept_ref[least_ref[i]]
        out_ref[NAMED * i + 1] = kept_ref[last_ref[i]]


def select_blocks(least, last, kept):
    count = NAMED * least.shape[0]
    vmem = pl.BlockSpec(memory_space=pltpu.VMEM)
    return pl.pallas_call(
        select_kernel,
        grid_spec=pltpu.PrefetchScalarGridSpec(
            num_scalar_prefetch=2, grid=(), in_specs=[vmem], out_specs=vmem
        ),
        out_shape=pltpu.VMEM((count,) + kept.shape[1:], kept.dtype),
        compiler_params=pltpu.CompilerParams(vmem_limit_bytes=4 * 1024 * 1024),
        name="select_blocks",
    )(least, last, kept)


def image_kernel(first_ref, block_ref, low_ref, high_ref, interp_ref, turns_ref, near_cos, near_sin, far_cos, far_sin, out_ref, mixed):
    blocks, rows, window = interp_ref.shape
    pulses = low_ref.shape[1] // 2
    span = low_ref.shape[2]
    scaling = 1.0 / math.sqrt(blocks * pulses)
    for k in range(blocks):
        samples = (low_ref[k] if k < blocks // 2 else high_ref[k - blocks // 2]).astype(jnp.float32)
        samples = pltpu.roll(samples, span - first_ref[k], 1)[:, :window].astype(jnp.bfloat16)
        product = lax.dot_general(
            interp_ref[block_ref[k]], samples, (((1,), (1,)), ((), ())), preferred_element_type=jnp.float32
        ).astype(jnp.bfloat16)
        mixed[0:rows, k * pulses:(k + 1) * pulses] = product[:, :pulses]
        mixed[rows:2 * rows, k * pulses:(k + 1) * pulses] = product[:, pulses:]
    real = mixed[0:rows].astype(jnp.float32) * scaling
    imag = mixed[rows:2 * rows].astype(jnp.float32) * scaling
    for q in range(QUARTERS):
        cosine, sine = turns_ref[2 * q:2 * q + 1], turns_ref[2 * q + 1:2 * q + 2]
        mixed[2 * q * rows:(2 * q + 1) * rows] = (real * cosine - imag * sine).astype(jnp.bfloat16)
        mixed[(2 * q + 1) * rows:(2 * q + 2) * rows] = (real * sine + imag * cosine).astype(jnp.bfloat16)
    wide = 2 * LANES
    per_quarter = COLS // QUARTERS // FINE

    def step(j, carry):
        for part in range(FINE // wide):
            cosines, sines = [], []
            for half in range(2):
                k = part * 2 + half
                turn_cos = far_cos[j, :, k:k + 1]
                turn_sin = far_sin[j, :, k:k + 1]
                cosines.append((turn_cos * near_cos[...] - turn_sin * near_sin[...]).astype(jnp.bfloat16))
                sines.append((turn_sin * near_cos[...] + turn_cos * near_sin[...]).astype(jnp.bfloat16))
            by_cos = jnp.dot(mixed[...], jnp.concatenate(cosines, 1), preferred_element_type=jnp.float32)
            by_sin = jnp.dot(mixed[...], jnp.concatenate(sines, 1), preferred_element_type=jnp.float32)
            columns = slice(part * wide, (part + 1) * wide)
            for q in range(QUARTERS):
                top = slice(2 * q * rows, (2 * q + 1) * rows)
                low = slice((2 * q + 1) * rows, (2 * q + 2) * rows)
                out_ref[q * per_quarter + j, :, columns] = (by_cos[top] - by_sin[low]).astype(jnp.bfloat16)
                out_ref[STEPS + q * per_quarter + j, :, columns] = (by_sin[top] + by_cos[low]).astype(jnp.bfloat16)
        return carry

    lax.fori_loop(0, per_quarter, step, 0)


def image_of(first, block, low, high, interp, turns, near, far):
    rows = interp.shape[1]
    pulses = interp.shape[0] * low.shape[1] // 2
    vmem = pl.BlockSpec(memory_space=pltpu.VMEM)
    return pl.pallas_call(
        image_kernel,
        grid_spec=pltpu.PrefetchScalarGridSpec(
            num_scalar_prefetch=2,
            grid=(),
            in_specs=[vmem] * 8,
            out_specs=vmem,
            scratch_shapes=[pltpu.VMEM((2 * QUARTERS * rows, pulses), jnp.bfloat16)],
        ),
        out_shape=jax.ShapeDtypeStruct((2 * STEPS, rows, FINE), jnp.bfloat16),
        compiler_params=pltpu.CompilerParams(vmem_limit_bytes=12 * 1024 * 1024),
        cost_estimate=pl.CostEstimate(
            flops=4 * rows * pulses * 2 * COLS, bytes_accessed=16 * 1024 * 1024, transcendentals=0
        ),
        name="image_rows",
    )(first, block, low, high, interp, turns, *near, *far)


def frame_kernel(place_ref, recv_ref, table_ref, image_ref, out_ref, staged, sems):
    rows = out_ref.shape[0]
    fine = table_ref.shape[2]
    per_step = FINE // fine

    def write(s):
        columns = pl.ds(pl.multiple_of(s * FINE, FINE), FINE)
        return pltpu.make_async_copy(staged.at[s], out_ref.at[:, columns], sems.at[s])

    def step(j, carry):
        blocks = [recv_ref[place_ref[j * per_step + i]] for i in range(per_step)]
        coarse = jnp.concatenate(blocks, 0)
        for part in range(2):
            kept_part = jnp.dot(coarse, table_ref[part], preferred_element_type=jnp.float32)
            s = part * STEPS + j
            for i in range(per_step):
                columns = slice(i * fine, (i + 1) * fine)
                staged[s, :, columns] = (
                    image_ref[s, :, columns] + kept_part[i * rows:(i + 1) * rows]
                ).astype(jnp.bfloat16)
            write(s).start()
        return carry

    lax.fori_loop(0, STEPS, step, 0, unroll=True)
    for s in range(2 * STEPS):
        write(s).wait()


def frame_of(place, recv, tables, image):
    rows = recv.shape[1]
    vmem = pl.BlockSpec(memory_space=pltpu.VMEM)
    return pl.pallas_call(
        frame_kernel,
        grid_spec=pltpu.PrefetchScalarGridSpec(
            num_scalar_prefetch=1,
            grid=(),
            in_specs=[vmem] * 3,
            out_specs=pl.BlockSpec(memory_space=pl.ANY),
            scratch_shapes=[
                pltpu.VMEM((2 * STEPS, rows, FINE), jnp.bfloat16),
                pltpu.SemaphoreType.DMA((2 * STEPS,)),
            ],
        ),
        out_shape=jax.ShapeDtypeStruct((rows, 2 * COLS), jnp.bfloat16),
        compiler_params=pltpu.CompilerParams(vmem_limit_bytes=12 * 1024 * 1024),
        name="frame_rows",
    )(place, recv, tables, image)


def trade(cells, bit):
    count = lax.axis_size("loop")
    return lax.ppermute(cells, "loop", [(i, i ^ bit) for i in range(count)])


def body(echoes, interp, offsets, wave, kept, lists):
    tiles = lax.axis_size("tile")
    loops = lax.axis_size("loop")
    my_tile = lax.axis_index("tile")
    my_loop = lax.axis_index("loop")
    slots, rows, samples = kept.shape
    count = lists.shape[1]
    pulse_block, bins_dev = echoes.shape[1:]
    window = interp.shape[2]
    bin_span = bins_dev // loops
    rim = window // 2 - bin_span // 2 + DRIFT

    owners = lists // (slots * loops)
    order = jnp.arange(count, dtype=jnp.int32)[None, :] * slots + lists % slots
    mine = owners == my_tile
    least = jnp.min(jnp.where(mine, order, count * slots), axis=1) % slots
    last = jnp.max(jnp.where(mine, order, 0), axis=1) % slots
    send = select_blocks(least, last, kept)
    recv = lax.all_to_all(
        send.reshape(tiles, NAMED, rows, samples), "tile", 0, 0, tiled=True
    ).reshape(tiles * NAMED, rows, samples)

    ends = tiles - 1
    before = lax.ppermute(echoes[:, :, bins_dev - rim:], "tile", [(i, i + 1) for i in range(ends)])
    after = lax.ppermute(echoes[:, :, :rim], "tile", [(i + 1, i) for i in range(ends)])
    extended = jnp.concatenate([before, echoes, after], axis=2).reshape(1, 2 * pulse_block, bins_dev + 2 * rim)
    upper, pair = my_loop // 4, my_loop // 2 % 2
    half = bins_dev
    kept_half = lax.dynamic_slice_in_dim(extended, upper * 2 * LANES, half, 2)
    sent_half = lax.dynamic_slice_in_dim(extended, (1 - upper) * 2 * LANES, half, 2)
    two = jnp.concatenate([kept_half, trade(sent_half, 4)], 0)
    reach = 3 * LANES
    kept_reach = lax.dynamic_slice_in_dim(two, pair * LANES, reach, 2)
    sent_reach = lax.dynamic_slice_in_dim(two, (1 - pair) * LANES, reach, 2)
    low = jnp.concatenate([kept_reach, trade(sent_reach, 2)], 0)
    high = trade(low, 1)
    block = my_loop ^ jnp.array([0, 4, 2, 6, 1, 5, 3, 7], jnp.int32)
    first = offsets[:, 0] - (my_tile * bins_dev - rim + my_loop // 2 * LANES)
    first = first[block]

    turned = wave.reshape(loops, pulse_block)[block].reshape(-1)
    near = turn(turned, jnp.arange(LANES, dtype=jnp.int32))
    far_count = COLS // QUARTERS // LANES
    far = turn(turned, jnp.arange(far_count, dtype=jnp.int32) * LANES)
    far = [x.reshape(-1, far_count * LANES // FINE, FINE // LANES).transpose(1, 0, 2) for x in far]
    turns = []
    for q in range(QUARTERS):
        quarter = turned * q % 4
        turns.append(jnp.where(quarter % 2 == 0, 1 - quarter, 0))
        turns.append(jnp.where(quarter % 2 == 1, 2 - quarter, 0))
    turns = jnp.stack(turns, 0).astype(jnp.float32)
    image = image_of(first, block, low, high, interp, turns, near, far)

    my_owners = lax.dynamic_index_in_dim(owners, my_tile, 0, keepdims=False)
    ids = jnp.arange(count, dtype=jnp.int32)
    earlier = (my_owners[:, None] == my_owners[None, :]) & (ids[None, :] < ids[:, None])
    place = my_owners * NAMED + jnp.any(earlier, axis=1).astype(jnp.int32)
    table = upsample_table(samples // 2, COLS // count)
    blank = jnp.zeros_like(table)
    tables = jnp.stack([jnp.concatenate([table, blank], 0), jnp.concatenate([blank, table], 0)], 0)
    return frame_of(place, recv, tables, image)


def solution(mesh):
    placed = (
        P(None, "loop", "tile"),
        P(None, ("tile", "loop"), None),
        P(None, ("tile", "loop")),
        P(),
        P(("tile", "loop"), None, None),
        P(None, "loop"),
    )
    return jax.shard_map(
        body, mesh=mesh, in_specs=placed, out_specs=P(("tile", "loop"), None), check_vma=False
    )
```

```python
import math

import jax
import jax.numpy as jnp
from jax import lax
from jax.experimental import pallas as pl
from jax.experimental.pallas import tpu as pltpu
from jax.sharding import PartitionSpec as P

COLS = 16384
DRIFT = 32
NAMED = 2
LANES = 128
STEPS = 16
FINE = 1024
QUARTERS = 4


def upsample_table(coarse, fine):
    factor = fine // coarse
    fine_ids = jnp.arange(fine, dtype=jnp.int32)
    lower_ids = fine_ids // factor
    upper_ids = jnp.minimum(lower_ids + 1, coarse - 1)
    fraction = (fine_ids % factor).astype(jnp.float32) / factor
    coarse_ids = jnp.arange(coarse, dtype=jnp.int32)[:, None]
    up_table = jnp.where(coarse_ids == lower_ids[None, :], 1.0 - fraction[None, :], 0.0)
    up_table = up_table + jnp.where(coarse_ids == upper_ids[None, :], fraction[None, :], 0.0)
    return up_table.astype(jnp.bfloat16)


def turn(wave, column_ids):
    phase = (wave[:, None] * column_ids[None, :] % COLS).astype(jnp.float32) * (2.0 * math.pi / COLS)
    return jnp.cos(phase), jnp.sin(phase)


def select_kernel(code_ref, kept_ref, out_ref):
    for i in range(out_ref.shape[0] // NAMED):
        code = jnp.maximum(code_ref[i], 1)
        lower = (31 - lax.clz(code & -code)) // 2
        upper = (31 - lax.clz(code)) // 2
        out_ref[NAMED * i] = kept_ref[lower]
        out_ref[NAMED * i + 1] = kept_ref[upper]


def select_blocks(code, kept):
    count = NAMED * code.shape[0]
    vmem = pl.BlockSpec(memory_space=pltpu.VMEM)
    return pl.pallas_call(
        select_kernel,
        grid_spec=pltpu.PrefetchScalarGridSpec(
            num_scalar_prefetch=1, grid=(), in_specs=[vmem], out_specs=vmem
        ),
        out_shape=pltpu.VMEM((count,) + kept.shape[1:], kept.dtype),
        compiler_params=pltpu.CompilerParams(vmem_limit_bytes=4 * 1024 * 1024),
        name="select_blocks",
    )(code, kept)


def image_kernel(first_ref, block_ref, low_ref, high_ref, interp_ref, turns_ref, near_cos, near_sin, far_cos, far_sin, out_ref, mixed):
    blocks, rows, window = interp_ref.shape
    pulses = low_ref.shape[1] // 2
    span = low_ref.shape[2]
    scaling = 1.0 / math.sqrt(blocks * pulses)
    for k in range(blocks):
        samples = (low_ref[k] if k < blocks // 2 else high_ref[k - blocks // 2]).astype(jnp.float32)
        samples = pltpu.roll(samples, span - first_ref[k], 1)[:, :window].astype(jnp.bfloat16)
        product = lax.dot_general(
            interp_ref[block_ref[k]], samples, (((1,), (1,)), ((), ())), preferred_element_type=jnp.float32
        ).astype(jnp.bfloat16)
        mixed[0:rows, k * pulses:(k + 1) * pulses] = product[:, :pulses]
        mixed[rows:2 * rows, k * pulses:(k + 1) * pulses] = product[:, pulses:]
    real = mixed[0:rows].astype(jnp.float32) * scaling
    imag = mixed[rows:2 * rows].astype(jnp.float32) * scaling
    for q in range(QUARTERS):
        cosine, sine = turns_ref[2 * q:2 * q + 1], turns_ref[2 * q + 1:2 * q + 2]
        mixed[2 * q * rows:(2 * q + 1) * rows] = (real * cosine - imag * sine).astype(jnp.bfloat16)
        mixed[(2 * q + 1) * rows:(2 * q + 2) * rows] = (real * sine + imag * cosine).astype(jnp.bfloat16)
    wide = 2 * LANES
    per_quarter = COLS // QUARTERS // FINE

    def step(j, carry):
        for part in range(FINE // wide):
            cosines, sines = [], []
            for half in range(2):
                k = part * 2 + half
                turn_cos = far_cos[j, :, k:k + 1]
                turn_sin = far_sin[j, :, k:k + 1]
                cosines.append((turn_cos * near_cos[...] - turn_sin * near_sin[...]).astype(jnp.bfloat16))
                sines.append((turn_sin * near_cos[...] + turn_cos * near_sin[...]).astype(jnp.bfloat16))
            by_cos = jnp.dot(mixed[...], jnp.concatenate(cosines, 1), preferred_element_type=jnp.float32)
            by_sin = jnp.dot(mixed[...], jnp.concatenate(sines, 1), preferred_element_type=jnp.float32)
            columns = slice(part * wide, (part + 1) * wide)
            for q in range(QUARTERS):
                top = slice(2 * q * rows, (2 * q + 1) * rows)
                low = slice((2 * q + 1) * rows, (2 * q + 2) * rows)
                out_ref[q * per_quarter + j, :, columns] = (by_cos[top] - by_sin[low]).astype(jnp.bfloat16)
                out_ref[STEPS + q * per_quarter + j, :, columns] = (by_sin[top] + by_cos[low]).astype(jnp.bfloat16)
        return carry

    lax.fori_loop(0, per_quarter, step, 0)


def image_of(first, block, low, high, interp, turns, near, far):
    rows = interp.shape[1]
    pulses = interp.shape[0] * low.shape[1] // 2
    vmem = pl.BlockSpec(memory_space=pltpu.VMEM)
    return pl.pallas_call(
        image_kernel,
        grid_spec=pltpu.PrefetchScalarGridSpec(
            num_scalar_prefetch=2,
            grid=(),
            in_specs=[vmem] * 8,
            out_specs=vmem,
            scratch_shapes=[pltpu.VMEM((2 * QUARTERS * rows, pulses), jnp.bfloat16)],
        ),
        out_shape=jax.ShapeDtypeStruct((2 * STEPS, rows, FINE), jnp.bfloat16),
        compiler_params=pltpu.CompilerParams(vmem_limit_bytes=12 * 1024 * 1024),
        cost_estimate=pl.CostEstimate(
            flops=4 * rows * pulses * 2 * COLS, bytes_accessed=16 * 1024 * 1024, transcendentals=0
        ),
        name="image_rows",
    )(first, block, low, high, interp, turns, *near, *far)


def frame_kernel(place_ref, recv_ref, table_ref, image_ref, out_ref, staged, sems):
    rows = out_ref.shape[0]
    fine = table_ref.shape[2]
    per_step = FINE // fine

    def write(s):
        columns = pl.ds(pl.multiple_of(s * FINE, FINE), FINE)
        return pltpu.make_async_copy(staged.at[s], out_ref.at[:, columns], sems.at[s])

    def step(j, carry):
        blocks = [recv_ref[place_ref[j * per_step + i]] for i in range(per_step)]
        coarse = jnp.concatenate(blocks, 0)
        for part in range(2):
            kept_part = jnp.dot(coarse, table_ref[part], preferred_element_type=jnp.float32)
            s = part * STEPS + j
            for i in range(per_step):
                columns = slice(i * fine, (i + 1) * fine)
                staged[s, :, columns] = (
                    image_ref[s, :, columns] + kept_part[i * rows:(i + 1) * rows]
                ).astype(jnp.bfloat16)
            write(s).start()
        return carry

    lax.fori_loop(0, STEPS, step, 0, unroll=True)
    for s in range(2 * STEPS):
        write(s).wait()


def frame_of(place, recv, tables, image):
    rows = recv.shape[1]
    vmem = pl.BlockSpec(memory_space=pltpu.VMEM)
    return pl.pallas_call(
        frame_kernel,
        grid_spec=pltpu.PrefetchScalarGridSpec(
            num_scalar_prefetch=1,
            grid=(),
            in_specs=[vmem] * 3,
            out_specs=pl.BlockSpec(memory_space=pl.ANY),
            scratch_shapes=[
                pltpu.VMEM((2 * STEPS, rows, FINE), jnp.bfloat16),
                pltpu.SemaphoreType.DMA((2 * STEPS,)),
            ],
        ),
        out_shape=jax.ShapeDtypeStruct((rows, 2 * COLS), jnp.bfloat16),
        compiler_params=pltpu.CompilerParams(vmem_limit_bytes=12 * 1024 * 1024),
        name="frame_rows",
    )(place, recv, tables, image)


def trade(cells, bit):
    count = lax.axis_size("loop")
    return lax.ppermute(cells, "loop", [(i, i ^ bit) for i in range(count)])


def body(echoes, interp, offsets, wave, kept, lists):
    tiles = lax.axis_size("tile")
    loops = lax.axis_size("loop")
    my_tile = lax.axis_index("tile")
    my_loop = lax.axis_index("loop")
    slots, rows, samples = kept.shape
    count = lists.shape[1]
    pulse_block, bins_dev = echoes.shape[1:]
    window = interp.shape[2]
    bin_span = bins_dev // loops
    rim = window // 2 - bin_span // 2 + DRIFT

    mine = lax.div(lists, jnp.int32(slots * loops)) == my_tile
    weight = lax.shift_left(jnp.int32(1), NAMED * lax.rem(lists, jnp.int32(slots)))
    code = jnp.sum(jnp.where(mine, weight, 0), axis=1)
    send = select_blocks(code, kept)
    recv = lax.all_to_all(
        send.reshape(tiles, NAMED, rows, samples), "tile", 0, 0, tiled=True
    ).reshape(tiles * NAMED, rows, samples)

    odd = my_tile % 2 == 1
    head, tail = echoes[:, :, :rim], echoes[:, :, bins_dev - rim:]
    outer = [(i, i + 1) for i in range(1, tiles - 1, 2)]
    inner = [(i, i + 1) for i in range(0, tiles, 2)]
    swap = lambda cells, pairs: lax.ppermute(cells, "tile", pairs + [(j, i) for i, j in pairs])
    across = swap(jnp.where(odd, tail, head), outer)
    beside, _ = lax.optimization_barrier((jnp.where(odd, head, tail), send))
    beside = swap(beside, inner)
    before, after = jnp.where(odd, beside, across), jnp.where(odd, across, beside)
    extended = jnp.concatenate([before, echoes, after], axis=2).reshape(1, 2 * pulse_block, bins_dev + 2 * rim)
    upper, pair = my_loop // 4, my_loop // 2 % 2
    half = bins_dev
    kept_half = lax.dynamic_slice_in_dim(extended, upper * 2 * LANES, half, 2)
    sent_half = lax.dynamic_slice_in_dim(extended, (1 - upper) * 2 * LANES, half, 2)
    two = jnp.concatenate([kept_half, trade(sent_half, 4)], 0)
    reach = 3 * LANES
    kept_reach = lax.dynamic_slice_in_dim(two, pair * LANES, reach, 2)
    sent_reach = lax.dynamic_slice_in_dim(two, (1 - pair) * LANES, reach, 2)
    low = jnp.concatenate([kept_reach, trade(sent_reach, 2)], 0)
    high = trade(low, 1)
    block = my_loop ^ jnp.array([0, 4, 2, 6, 1, 5, 3, 7], jnp.int32)
    first = offsets[:, 0] - (my_tile * bins_dev - rim + my_loop // 2 * LANES)
    first = first[block]

    turned = wave.reshape(loops, pulse_block)[block].reshape(-1)
    near = turn(turned, jnp.arange(LANES, dtype=jnp.int32))
    far_count = COLS // QUARTERS // LANES
    far = turn(turned, jnp.arange(far_count, dtype=jnp.int32) * LANES)
    far = [x.reshape(-1, far_count * LANES // FINE, FINE // LANES).transpose(1, 0, 2) for x in far]
    turns = []
    for q in range(QUARTERS):
        quarter = turned * q % 4
        turns.append(jnp.where(quarter % 2 == 0, 1 - quarter, 0))
        turns.append(jnp.where(quarter % 2 == 1, 2 - quarter, 0))
    turns = jnp.stack(turns, 0).astype(jnp.float32)
    image = image_of(first, block, low, high, interp, turns, near, far)

    my_list = lax.dynamic_index_in_dim(lists, my_tile, 0, keepdims=False)
    my_owners, my_slots = my_list // (slots * loops), my_list % slots
    lower = (my_owners[:, None] == my_owners[None, :]) & (my_slots[None, :] < my_slots[:, None])
    place = my_owners * NAMED + jnp.any(lower, axis=1).astype(jnp.int32)
    table = upsample_table(samples // 2, COLS // count)
    blank = jnp.zeros_like(table)
    tables = jnp.stack([jnp.concatenate([table, blank], 0), jnp.concatenate([blank, table], 0)], 0)
    return frame_of(place, recv, tables, image)


def solution(mesh):
    placed = (
        P(None, "loop", "tile"),
        P(None, ("tile", "loop"), None),
        P(None, ("tile", "loop")),
        P(),
        P(("tile", "loop"), None, None),
        P(None, "loop"),
    )
    return jax.shard_map(
        body, mesh=mesh, in_specs=placed, out_specs=P(("tile", "loop"), None), check_vma=False
    )
```

```python
import math

import jax
import jax.numpy as jnp
from jax import lax
from jax.experimental import pallas as pl
from jax.experimental.pallas import tpu as pltpu
from jax.sharding import PartitionSpec as P

COLS = 16384
DRIFT = 32
NAMED = 2
LANES = 128
STEPS = 16
FINE = 1024
QUARTERS = 4
ORDER = (19, 1, 13, 8, 3, 23, 11, 12, 18, 14, 15, 10, 17, 31, 0, 30,
         6, 2, 22, 26, 27, 24, 4, 28, 7, 20, 5, 25, 29, 21, 9, 16)


def upsample_table(coarse, fine):
    factor = fine // coarse
    fine_ids = jnp.arange(fine, dtype=jnp.int32)
    lower_ids = fine_ids // factor
    upper_ids = jnp.minimum(lower_ids + 1, coarse - 1)
    fraction = (fine_ids % factor).astype(jnp.float32) / factor
    coarse_ids = jnp.arange(coarse, dtype=jnp.int32)[:, None]
    up_table = jnp.where(coarse_ids == lower_ids[None, :], 1.0 - fraction[None, :], 0.0)
    up_table = up_table + jnp.where(coarse_ids == upper_ids[None, :], fraction[None, :], 0.0)
    return up_table.astype(jnp.bfloat16)


def turn(wave, column_ids):
    phase = (wave[:, None] * column_ids[None, :] % COLS).astype(jnp.float32) * (2.0 * math.pi / COLS)
    return jnp.cos(phase), jnp.sin(phase)


def select_kernel(code_ref, kept_ref, out_ref):
    for i in range(out_ref.shape[0] // NAMED):
        code = jnp.maximum(code_ref[ORDER[i]], 1)
        lower = (31 - lax.clz(code & -code)) // 2
        upper = (31 - lax.clz(code)) // 2
        out_ref[NAMED * i] = kept_ref[lower]
        out_ref[NAMED * i + 1] = kept_ref[upper]


def select_blocks(code, kept):
    count = NAMED * code.shape[0]
    vmem = pl.BlockSpec(memory_space=pltpu.VMEM)
    return pl.pallas_call(
        select_kernel,
        grid_spec=pltpu.PrefetchScalarGridSpec(
            num_scalar_prefetch=1, grid=(), in_specs=[vmem], out_specs=vmem
        ),
        out_shape=pltpu.VMEM((count,) + kept.shape[1:], kept.dtype),
        compiler_params=pltpu.CompilerParams(vmem_limit_bytes=4 * 1024 * 1024),
        name="select_blocks",
    )(code, kept)


def image_kernel(first_ref, block_ref, low_ref, high_ref, interp_ref, turns_ref, near_cos, near_sin, far_cos, far_sin, out_ref, mixed):
    blocks, rows, window = interp_ref.shape
    pulses = low_ref.shape[1] // 2
    span = low_ref.shape[2]
    scaling = 1.0 / math.sqrt(blocks * pulses)
    for k in range(blocks):
        samples = (low_ref[k] if k < blocks // 2 else high_ref[k - blocks // 2]).astype(jnp.float32)
        samples = pltpu.roll(samples, span - first_ref[k], 1)[:, :window].astype(jnp.bfloat16)
        product = lax.dot_general(
            interp_ref[block_ref[k]], samples, (((1,), (1,)), ((), ())), preferred_element_type=jnp.float32
        ).astype(jnp.bfloat16)
        mixed[0:rows, k * pulses:(k + 1) * pulses] = product[:, :pulses]
        mixed[rows:2 * rows, k * pulses:(k + 1) * pulses] = product[:, pulses:]
    real = mixed[0:rows].astype(jnp.float32) * scaling
    imag = mixed[rows:2 * rows].astype(jnp.float32) * scaling
    for q in range(QUARTERS):
        cosine, sine = turns_ref[2 * q:2 * q + 1], turns_ref[2 * q + 1:2 * q + 2]
        mixed[2 * q * rows:(2 * q + 1) * rows] = (real * cosine - imag * sine).astype(jnp.bfloat16)
        mixed[(2 * q + 1) * rows:(2 * q + 2) * rows] = (real * sine + imag * cosine).astype(jnp.bfloat16)
    wide = 2 * LANES
    per_quarter = COLS // QUARTERS // FINE

    def step(j, carry):
        for part in range(FINE // wide):
            cosines, sines = [], []
            for half in range(2):
                k = part * 2 + half
                turn_cos = far_cos[j, :, k:k + 1]
                turn_sin = far_sin[j, :, k:k + 1]
                cosines.append((turn_cos * near_cos[...] - turn_sin * near_sin[...]).astype(jnp.bfloat16))
                sines.append((turn_sin * near_cos[...] + turn_cos * near_sin[...]).astype(jnp.bfloat16))
            by_cos = jnp.dot(mixed[...], jnp.concatenate(cosines, 1), preferred_element_type=jnp.float32)
            by_sin = jnp.dot(mixed[...], jnp.concatenate(sines, 1), preferred_element_type=jnp.float32)
            columns = slice(part * wide, (part + 1) * wide)
            for q in range(QUARTERS):
                top = slice(2 * q * rows, (2 * q + 1) * rows)
                low = slice((2 * q + 1) * rows, (2 * q + 2) * rows)
                out_ref[q * per_quarter + j, :, columns] = (by_cos[top] - by_sin[low]).astype(jnp.bfloat16)
                out_ref[STEPS + q * per_quarter + j, :, columns] = (by_sin[top] + by_cos[low]).astype(jnp.bfloat16)
        return carry

    lax.fori_loop(0, per_quarter, step, 0)


def image_of(first, block, low, high, interp, turns, near, far):
    rows = interp.shape[1]
    pulses = interp.shape[0] * low.shape[1] // 2
    vmem = pl.BlockSpec(memory_space=pltpu.VMEM)
    return pl.pallas_call(
        image_kernel,
        grid_spec=pltpu.PrefetchScalarGridSpec(
            num_scalar_prefetch=2,
            grid=(),
            in_specs=[vmem] * 8,
            out_specs=vmem,
            scratch_shapes=[pltpu.VMEM((2 * QUARTERS * rows, pulses), jnp.bfloat16)],
        ),
        out_shape=jax.ShapeDtypeStruct((2 * STEPS, rows, FINE), jnp.bfloat16),
        compiler_params=pltpu.CompilerParams(vmem_limit_bytes=12 * 1024 * 1024),
        cost_estimate=pl.CostEstimate(
            flops=4 * rows * pulses * 2 * COLS, bytes_accessed=16 * 1024 * 1024, transcendentals=0
        ),
        name="image_rows",
    )(first, block, low, high, interp, turns, *near, *far)


def frame_kernel(place_ref, recv_ref, table_ref, image_ref, out_ref, staged, sems):
    rows = out_ref.shape[0]
    fine = table_ref.shape[2]
    per_step = FINE // fine

    def write(s):
        columns = pl.ds(pl.multiple_of(s * FINE, FINE), FINE)
        return pltpu.make_async_copy(staged.at[s], out_ref.at[:, columns], sems.at[s])

    def step(j, carry):
        blocks = [recv_ref[place_ref[j * per_step + i]] for i in range(per_step)]
        coarse = jnp.concatenate(blocks, 0)
        for part in range(2):
            kept_part = jnp.dot(coarse, table_ref[part], preferred_element_type=jnp.float32)
            s = part * STEPS + j
            for i in range(per_step):
                columns = slice(i * fine, (i + 1) * fine)
                staged[s, :, columns] = (
                    image_ref[s, :, columns] + kept_part[i * rows:(i + 1) * rows]
                ).astype(jnp.bfloat16)
            write(s).start()
        return carry

    lax.fori_loop(0, STEPS, step, 0, unroll=True)
    for s in range(2 * STEPS):
        write(s).wait()


def frame_of(place, recv, tables, image):
    rows = recv.shape[1]
    vmem = pl.BlockSpec(memory_space=pltpu.VMEM)
    return pl.pallas_call(
        frame_kernel,
        grid_spec=pltpu.PrefetchScalarGridSpec(
            num_scalar_prefetch=1,
            grid=(),
            in_specs=[vmem] * 3,
            out_specs=pl.BlockSpec(memory_space=pl.ANY),
            scratch_shapes=[
                pltpu.VMEM((2 * STEPS, rows, FINE), jnp.bfloat16),
                pltpu.SemaphoreType.DMA((2 * STEPS,)),
            ],
        ),
        out_shape=jax.ShapeDtypeStruct((rows, 2 * COLS), jnp.bfloat16),
        compiler_params=pltpu.CompilerParams(vmem_limit_bytes=12 * 1024 * 1024),
        name="frame_rows",
    )(place, recv, tables, image)


def trade(cells, bit):
    count = lax.axis_size("loop")
    return lax.ppermute(cells, "loop", [(i, i ^ bit) for i in range(count)])


def body(echoes, interp, offsets, wave, kept, lists):
    tiles = lax.axis_size("tile")
    loops = lax.axis_size("loop")
    my_tile = lax.axis_index("tile")
    my_loop = lax.axis_index("loop")
    slots, rows, samples = kept.shape
    count = lists.shape[1]
    pulse_block, bins_dev = echoes.shape[1:]
    window = interp.shape[2]
    bin_span = bins_dev // loops
    rim = window // 2 - bin_span // 2 + DRIFT

    mine = lax.div(lists, jnp.int32(slots * loops)) == my_tile
    weight = lax.shift_left(jnp.int32(1), NAMED * lax.rem(lists, jnp.int32(slots)))
    code = jnp.sum(jnp.where(mine, weight, 0), axis=1)
    send = select_blocks(code, kept)
    recv = lax.all_to_all(
        send.reshape(tiles, NAMED, rows, samples), "tile", 0, 0, axis_index_groups=[list(ORDER)], tiled=True
    ).reshape(tiles * NAMED, rows, samples)

    my_list = lax.dynamic_index_in_dim(lists, my_tile, 0, keepdims=False)

    odd = my_tile % 2 == 1
    head, tail = echoes[:, :, :rim], echoes[:, :, bins_dev - rim:]
    outer = [(i, i + 1) for i in range(1, tiles - 1, 2)]
    inner = [(i, i + 1) for i in range(0, tiles, 2)]
    swap = lambda cells, pairs: lax.ppermute(cells, "tile", pairs + [(j, i) for i, j in pairs])
    across = swap(jnp.where(odd, tail, head), outer)
    beside, _ = lax.optimization_barrier((jnp.where(odd, head, tail), send))
    beside = swap(beside, inner)
    before, after = jnp.where(odd, beside, across), jnp.where(odd, across, beside)
    extended = jnp.concatenate([before, echoes, after], axis=2).reshape(1, 2 * pulse_block, bins_dev + 2 * rim)
    upper, pair = my_loop // 4, my_loop // 2 % 2
    half = bins_dev
    kept_half = lax.dynamic_slice_in_dim(extended, upper * 2 * LANES, half, 2)
    sent_half = lax.dynamic_slice_in_dim(extended, (1 - upper) * 2 * LANES, half, 2)
    sent_half, wave, offsets, my_list = lax.optimization_barrier((sent_half, wave, offsets, my_list))
    two = jnp.concatenate([kept_half, trade(sent_half, 4)], 0)
    reach = 3 * LANES
    kept_reach = lax.dynamic_slice_in_dim(two, pair * LANES, reach, 2)
    sent_reach = lax.dynamic_slice_in_dim(two, (1 - pair) * LANES, reach, 2)
    low = jnp.concatenate([kept_reach, trade(sent_reach, 2)], 0)
    high = trade(low, 1)
    block = my_loop ^ jnp.array([0, 4, 2, 6, 1, 5, 3, 7], jnp.int32)
    first = offsets[:, 0] - (my_tile * bins_dev - rim + my_loop // 2 * LANES)
    first = first[block]

    turned = wave.reshape(loops, pulse_block)[block].reshape(-1)
    near = turn(turned, jnp.arange(LANES, dtype=jnp.int32))
    far_count = COLS // QUARTERS // LANES
    far = turn(turned, jnp.arange(far_count, dtype=jnp.int32) * LANES)
    far = [x.reshape(-1, far_count * LANES // FINE, FINE // LANES).transpose(1, 0, 2) for x in far]
    turns = []
    for q in range(QUARTERS):
        quarter = turned * q % 4
        turns.append(jnp.where(quarter % 2 == 0, 1 - quarter, 0))
        turns.append(jnp.where(quarter % 2 == 1, 2 - quarter, 0))
    turns = jnp.stack(turns, 0).astype(jnp.float32)
    image = image_of(first, block, low, high, interp, turns, near, far)

    my_owners, my_slots = my_list // (slots * loops), my_list % slots
    lower = (my_owners[:, None] == my_owners[None, :]) & (my_slots[None, :] < my_slots[:, None])
    spots = jnp.arange(tiles, dtype=jnp.int32)
    spot = jnp.sum(jnp.where(my_owners[:, None] == jnp.array(ORDER, jnp.int32)[None, :], spots[None, :], 0), axis=1)
    place = spot * NAMED + jnp.any(lower, axis=1).astype(jnp.int32)
    table = upsample_table(samples // 2, COLS // count)
    blank = jnp.zeros_like(table)
    tables = jnp.stack([jnp.concatenate([table, blank], 0), jnp.concatenate([blank, table], 0)], 0)
    return frame_of(place, recv, tables, image)


def solution(mesh):
    placed = (
        P(None, "loop", "tile"),
        P(None, ("tile", "loop"), None),
        P(None, ("tile", "loop")),
        P(),
        P(("tile", "loop"), None, None),
        P(None, "loop"),
    )
    return jax.shard_map(
        body, mesh=mesh, in_specs=placed, out_specs=P(("tile", "loop"), None), check_vma=False
    )
```

```python
import math

import jax
import jax.numpy as jnp
from jax import lax
from jax.experimental import pallas as pl
from jax.experimental.pallas import tpu as pltpu
from jax.sharding import PartitionSpec as P

COLS = 16384
DRIFT = 32
NAMED = 2
LANES = 128
STEPS = 16
FINE = 1024
QUARTERS = 4
LAST = 4
ORDER = (19, 1, 13, 8, 3, 23, 11, 12, 18, 14, 15, 10, 17, 31, 0, 30,
         6, 2, 22, 26, 27, 24, 4, 28, 7, 20, 5, 25, 29, 21, 9, 16)


def upsample_table(coarse, fine):
    factor = fine // coarse
    fine_ids = jnp.arange(fine, dtype=jnp.int32)
    lower_ids = fine_ids // factor
    upper_ids = jnp.minimum(lower_ids + 1, coarse - 1)
    fraction = (fine_ids % factor).astype(jnp.float32) / factor
    coarse_ids = jnp.arange(coarse, dtype=jnp.int32)[:, None]
    up_table = jnp.where(coarse_ids == lower_ids[None, :], 1.0 - fraction[None, :], 0.0)
    up_table = up_table + jnp.where(coarse_ids == upper_ids[None, :], fraction[None, :], 0.0)
    return up_table.astype(jnp.bfloat16)


def turn(wave, column_ids):
    phase = (wave[:, None] * column_ids[None, :] % COLS).astype(jnp.float32) * (2.0 * math.pi / COLS)
    return jnp.cos(phase), jnp.sin(phase)


def select_kernel(code_ref, kept_ref, out_ref):
    for i in range(out_ref.shape[0] // NAMED):
        code = jnp.maximum(code_ref[ORDER[i]], 1)
        lower = (31 - lax.clz(code & -code)) // 2
        upper = (31 - lax.clz(code)) // 2
        out_ref[NAMED * i] = kept_ref[lower]
        out_ref[NAMED * i + 1] = kept_ref[upper]


def select_blocks(code, kept):
    count = NAMED * code.shape[0]
    vmem = pl.BlockSpec(memory_space=pltpu.VMEM)
    return pl.pallas_call(
        select_kernel,
        grid_spec=pltpu.PrefetchScalarGridSpec(
            num_scalar_prefetch=1, grid=(), in_specs=[vmem], out_specs=vmem
        ),
        out_shape=pltpu.VMEM((count,) + kept.shape[1:], kept.dtype),
        compiler_params=pltpu.CompilerParams(vmem_limit_bytes=4 * 1024 * 1024),
        name="select_blocks",
    )(code, kept)


def image_kernel(first_ref, block_ref, low_ref, high_ref, interp_ref, turns_ref, near_cos, near_sin, far_cos, far_sin, out_ref, last_ref, mixed):
    blocks, rows, window = interp_ref.shape
    pulses = low_ref.shape[1] // 2
    span = low_ref.shape[2]
    scaling = 1.0 / math.sqrt(blocks * pulses)
    for k in range(blocks):
        samples = (low_ref[k] if k < blocks // 2 else high_ref[k - blocks // 2]).astype(jnp.float32)
        samples = pltpu.roll(samples, span - first_ref[k], 1)[:, :window].astype(jnp.bfloat16)
        product = lax.dot_general(
            interp_ref[block_ref[k]], samples, (((1,), (1,)), ((), ())), preferred_element_type=jnp.float32
        ).astype(jnp.bfloat16)
        mixed[0:rows, k * pulses:(k + 1) * pulses] = product[:, :pulses]
        mixed[rows:2 * rows, k * pulses:(k + 1) * pulses] = product[:, pulses:]
    real = mixed[0:rows].astype(jnp.float32) * scaling
    imag = mixed[rows:2 * rows].astype(jnp.float32) * scaling
    for q in range(QUARTERS):
        cosine, sine = turns_ref[2 * q:2 * q + 1], turns_ref[2 * q + 1:2 * q + 2]
        mixed[2 * q * rows:(2 * q + 1) * rows] = (real * cosine - imag * sine).astype(jnp.bfloat16)
        mixed[(2 * q + 1) * rows:(2 * q + 2) * rows] = (real * sine + imag * cosine).astype(jnp.bfloat16)
    wide = 2 * LANES
    per_quarter = COLS // QUARTERS // FINE

    def step(j, carry):
        for part in range(FINE // wide):
            cosines, sines = [], []
            for half in range(2):
                k = part * 2 + half
                turn_cos = far_cos[j, :, k:k + 1]
                turn_sin = far_sin[j, :, k:k + 1]
                cosines.append((turn_cos * near_cos[...] - turn_sin * near_sin[...]).astype(jnp.bfloat16))
                sines.append((turn_sin * near_cos[...] + turn_cos * near_sin[...]).astype(jnp.bfloat16))
            by_cos = jnp.dot(mixed[...], jnp.concatenate(cosines, 1), preferred_element_type=jnp.float32)
            by_sin = jnp.dot(mixed[...], jnp.concatenate(sines, 1), preferred_element_type=jnp.float32)
            columns = slice(part * wide, (part + 1) * wide)
            for q in range(QUARTERS):
                top = slice(2 * q * rows, (2 * q + 1) * rows)
                low = slice((2 * q + 1) * rows, (2 * q + 2) * rows)
                out_ref[q * per_quarter + j, :, columns] = (by_cos[top] - by_sin[low]).astype(jnp.bfloat16)
                ending = (by_sin[top] + by_cos[low]).astype(jnp.bfloat16)
                if q < QUARTERS - 1:
                    out_ref[STEPS + q * per_quarter + j, :, columns] = ending
                else:
                    last_ref[j, :, columns] = ending
        return carry

    lax.fori_loop(0, per_quarter, step, 0)


def image_of(first, block, low, high, interp, turns, near, far):
    rows = interp.shape[1]
    pulses = interp.shape[0] * low.shape[1] // 2
    vmem = pl.BlockSpec(memory_space=pltpu.VMEM)
    return pl.pallas_call(
        image_kernel,
        grid_spec=pltpu.PrefetchScalarGridSpec(
            num_scalar_prefetch=2,
            grid=(),
            in_specs=[vmem] * 8,
            out_specs=[vmem, vmem],
            scratch_shapes=[pltpu.VMEM((2 * QUARTERS * rows, pulses), jnp.bfloat16)],
        ),
        out_shape=[
            jax.ShapeDtypeStruct((2 * STEPS - LAST, rows, FINE), jnp.bfloat16),
            jax.ShapeDtypeStruct((LAST, rows, FINE), jnp.bfloat16),
        ],
        compiler_params=pltpu.CompilerParams(vmem_limit_bytes=12 * 1024 * 1024),
        cost_estimate=pl.CostEstimate(
            flops=4 * rows * pulses * 2 * COLS, bytes_accessed=16 * 1024 * 1024, transcendentals=0
        ),
        name="image_rows",
    )(first, block, low, high, interp, turns, *near, *far)


def frame_kernel(place_ref, recv_ref, table_ref, image_ref, last_ref, out_ref, staged, sems):
    rows = out_ref.shape[0]
    fine = table_ref.shape[2]
    per_step = FINE // fine

    def write(s):
        columns = pl.ds(s * FINE, FINE)
        return pltpu.make_async_copy(staged.at[s], out_ref.at[:, columns], sems.at[s])

    for j in range(STEPS):
        blocks = [recv_ref[place_ref[j * per_step + i]] for i in range(per_step)]
        coarse = jnp.concatenate(blocks, 0)
        for part in range(2):
            kept_part = jnp.dot(coarse, table_ref[part], preferred_element_type=jnp.float32)
            s = part * STEPS + j
            source = image_ref.at[s] if s < 2 * STEPS - LAST else last_ref.at[s - 2 * STEPS + LAST]
            for i in range(per_step):
                columns = slice(i * fine, (i + 1) * fine)
                staged[s, :, columns] = (
                    source[:, columns] + kept_part[i * rows:(i + 1) * rows]
                ).astype(jnp.bfloat16)
            write(s).start()
    for s in range(2 * STEPS):
        write(s).wait()


def frame_of(place, recv, tables, image):
    rows = recv.shape[1]
    vmem = pl.BlockSpec(memory_space=pltpu.VMEM)
    return pl.pallas_call(
        frame_kernel,
        grid_spec=pltpu.PrefetchScalarGridSpec(
            num_scalar_prefetch=1,
            grid=(),
            in_specs=[vmem] * 4,
            out_specs=pl.BlockSpec(memory_space=pl.ANY),
            scratch_shapes=[
                pltpu.VMEM((2 * STEPS, rows, FINE), jnp.bfloat16),
                pltpu.SemaphoreType.DMA((2 * STEPS,)),
            ],
        ),
        out_shape=jax.ShapeDtypeStruct((rows, 2 * COLS), jnp.bfloat16),
        compiler_params=pltpu.CompilerParams(vmem_limit_bytes=12 * 1024 * 1024),
        name="frame_rows",
    )(place, recv, tables, *image)


def trade(cells, bit):
    count = lax.axis_size("loop")
    return lax.ppermute(cells, "loop", [(i, i ^ bit) for i in range(count)])


def body(echoes, interp, offsets, wave, kept, lists):
    tiles = lax.axis_size("tile")
    loops = lax.axis_size("loop")
    my_tile = lax.axis_index("tile")
    my_loop = lax.axis_index("loop")
    slots, rows, samples = kept.shape
    count = lists.shape[1]
    pulse_block, bins_dev = echoes.shape[1:]
    window = interp.shape[2]
    bin_span = bins_dev // loops
    rim = window // 2 - bin_span // 2 + DRIFT

    mine = lax.div(lists, jnp.int32(slots * loops)) == my_tile
    weight = lax.shift_left(jnp.int32(1), NAMED * lax.rem(lists, jnp.int32(slots)))
    code = jnp.sum(jnp.where(mine, weight, 0), axis=1)
    send = select_blocks(code, kept)
    recv = lax.all_to_all(
        send.reshape(tiles, NAMED, rows, samples), "tile", 0, 0, axis_index_groups=[list(ORDER)], tiled=True
    ).reshape(tiles * NAMED, rows, samples)

    my_list = lax.dynamic_index_in_dim(lists, my_tile, 0, keepdims=False)

    odd = my_tile % 2 == 1
    head, tail = echoes[:, :, :rim], echoes[:, :, bins_dev - rim:]
    outer = [(i, i + 1) for i in range(1, tiles - 1, 2)]
    inner = [(i, i + 1) for i in range(0, tiles, 2)]
    swap = lambda cells, pairs: lax.ppermute(cells, "tile", pairs + [(j, i) for i, j in pairs])
    across = swap(jnp.where(odd, tail, head), outer)
    beside, _ = lax.optimization_barrier((jnp.where(odd, head, tail), send))
    beside = swap(beside, inner)
    before, after = jnp.where(odd, beside, across), jnp.where(odd, across, beside)
    extended = jnp.concatenate([before, echoes, after], axis=2).reshape(1, 2 * pulse_block, bins_dev + 2 * rim)
    upper, pair = my_loop // 4, my_loop // 2 % 2
    half = bins_dev
    kept_half = lax.dynamic_slice_in_dim(extended, upper * 2 * LANES, half, 2)
    sent_half = lax.dynamic_slice_in_dim(extended, (1 - upper) * 2 * LANES, half, 2)
    sent_half, wave, offsets, my_list = lax.optimization_barrier((sent_half, wave, offsets, my_list))
    two = jnp.concatenate([kept_half, trade(sent_half, 4)], 0)
    reach = 3 * LANES
    kept_reach = lax.dynamic_slice_in_dim(two, pair * LANES, reach, 2)
    sent_reach = lax.dynamic_slice_in_dim(two, (1 - pair) * LANES, reach, 2)
    low = jnp.concatenate([kept_reach, trade(sent_reach, 2)], 0)
    high = trade(low, 1)
    block = my_loop ^ jnp.array([0, 4, 2, 6, 1, 5, 3, 7], jnp.int32)
    first = offsets[:, 0] - (my_tile * bins_dev - rim + my_loop // 2 * LANES)
    first = first[block]

    turned = wave.reshape(loops, pulse_block)[block].reshape(-1)
    near = turn(turned, jnp.arange(LANES, dtype=jnp.int32))
    far_count = COLS // QUARTERS // LANES
    far = turn(turned, jnp.arange(far_count, dtype=jnp.int32) * LANES)
    far = [x.reshape(-1, far_count * LANES // FINE, FINE // LANES).transpose(1, 0, 2) for x in far]
    turns = []
    for q in range(QUARTERS):
        quarter = turned * q % 4
        turns.append(jnp.where(quarter % 2 == 0, 1 - quarter, 0))
        turns.append(jnp.where(quarter % 2 == 1, 2 - quarter, 0))
    turns = jnp.stack(turns, 0).astype(jnp.float32)
    image = image_of(first, block, low, high, interp, turns, near, far)

    my_owners, my_slots = my_list // (slots * loops), my_list % slots
    lower = (my_owners[:, None] == my_owners[None, :]) & (my_slots[None, :] < my_slots[:, None])
    spots = jnp.arange(tiles, dtype=jnp.int32)
    spot = jnp.sum(jnp.where(my_owners[:, None] == jnp.array(ORDER, jnp.int32)[None, :], spots[None, :], 0), axis=1)
    place = spot * NAMED + jnp.any(lower, axis=1).astype(jnp.int32)
    table = upsample_table(samples // 2, COLS // count)
    blank = jnp.zeros_like(table)
    tables = jnp.stack([jnp.concatenate([table, blank], 0), jnp.concatenate([blank, table], 0)], 0)
    return frame_of(place, recv, tables, image)


def solution(mesh):
    placed = (
        P(None, "loop", "tile"),
        P(None, ("tile", "loop"), None),
        P(None, ("tile", "loop")),
        P(),
        P(("tile", "loop"), None, None),
        P(None, "loop"),
    )
    return jax.shard_map(
        body, mesh=mesh, in_specs=placed, out_specs=P(("tile", "loop"), None), check_vma=False
    )
```
